768 devices in a mesh: row: 16 (over x_hi, y), col: 48 (over z, x_lo, core).
Axes of the slice: x: 4 (x_hi: 2, x_lo: 2; x = x_hi * 2 + x_lo), y: 8, z: 12, core: 2. Of those that a mesh axis runs over, the one named last changes fastest.
Arguments:
- features: float32 [98304, 256], P(('row', 'col')), may hold values from -6 to 6
- weight: float32 [256, 256], replicated, may hold values from -0.375 to 0.375
- cotangent: float32 [98304, 256], P(('row', 'col')), may hold values from -6 to 6
- tiles: float32 [16, 48, 16, 128, 128], P('row', 'col'), may hold values from -0.1875 to 0.1875
- tile_rows: int32 [16, 48, 16], P('row', 'col'), may hold values from -1 to 47, as said below
- tile_cols: int32 [16, 48, 16], P('row', 'col'), may hold values from 0 to 15, as said below
Outputs:
- hidden: float32 [98304, 256], P(('row', 'col'))
- grad_features: float32 [98304, 256], P(('row', 'col'))
- grad_weight: float32 [256, 256], replicated
The draws below stay inside these ranges and needn't reach their ends.
Inputs may be any that keep to these rules, and one draw needn't show every extreme that they name: `tile_rows`: -1 marks an empty slot; otherwise a block row of the slot's row group. Live slots come first on every device, the first slot of every device is live, and some device has all 16 slots live. Several slots may share a block row or a whole position, and a block row may have no tile. `tile_cols`: A block column of the column group may be absent from a device's live slots.
All inputs are finite; a program needn't handle non-finite values.
Results may differ from the reference program's by a relative error of at most 0.0003.
Values sent between devices are 32-bit elements; how exact they have to be, the bound alone decides.
A program may use at most 32 MiB of HBM per device.

```python
import jax
import jax.numpy as jnp
from jax import lax

FEAT = 256
BLOCK = 128
NODE_DEV = 128
SLOTS = 16
NODES = 98304
N_ROW = 16
N_COL = 48


def draw_tile_rows(key, part):
    key = jax.random.fold_in(key, 11)
    count_key, full_key, row_key = jax.random.split(key, 3)
    block_rows = N_COL * NODE_DEV // BLOCK
    devices = N_ROW * N_COL
    lowest = max(1, SLOTS // 4)
    highest = max(lowest + 1, 3 * SLOTS // 4 + 1)
    live_count = jax.random.randint(count_key, (devices,), lowest, highest)
    full_device = jax.random.randint(full_key, (), 0, devices)
    live_count = jnp.where(jnp.arange(devices) == full_device, SLOTS, live_count)
    slot_rows = jax.random.randint(row_key, (devices, SLOTS), 0, block_rows)
    slot_rows = jnp.where(jnp.arange(SLOTS)[None, :] < live_count[:, None], slot_rows, -1)
    return slot_rows.reshape(N_ROW, N_COL, SLOTS).astype(jnp.int32)


def draw_tile_cols(key, part):
    key = jax.random.fold_in(key, 23)
    block_cols = N_ROW * NODE_DEV // BLOCK
    slot_cols = jax.random.randint(key, (N_ROW, N_COL, SLOTS), 0, block_cols)
    return slot_cols.astype(jnp.int32)


def steps_of(own_key, extent, shards, least, largest):
    factor_of = 1.0
    for position, parts in shards:
        heights = jax.random.uniform(jax.random.fold_in(jax.random.fold_in(own_key, 6), position), (parts,), jnp.float32, least / len(shards), largest / len(shards))
        factor_of = factor_of * jnp.repeat(jnp.exp(heights), extent[position] // parts).reshape((-1,) + (1,) * (len(extent) - 1 - position))
    return factor_of


def bell_draw(rng, extent, spread, limit, cuts=(), held_as=jnp.bfloat16):
    gain = steps_of(rng, extent, cuts, -0.22, 0.18) if cuts else 1.0
    drawn = jax.random.normal(rng, extent, jnp.float32) * spread * gain
    return jnp.minimum(jnp.maximum(drawn, -limit), limit).astype(held_as)


def setup_inputs(seed: int = 0) -> dict:
    arg_keys = jax.random.split(jax.random.key(seed), 7)
    return {
        "features": bell_draw(arg_keys[0], (NODES, FEAT), 1.0, 6.0, ((0, 768),), jnp.float32),
        "weight": bell_draw(arg_keys[1], (FEAT, FEAT), FEAT ** -0.5, 0.375, (), jnp.float32),
        "cotangent": bell_draw(arg_keys[2], (NODES, FEAT), 1.0, 6.0, ((0, 768),), jnp.float32),
        "tiles": bell_draw(arg_keys[3], (N_ROW, N_COL, SLOTS, BLOCK, BLOCK), (BLOCK * SLOTS // 2) ** -0.5, 0.1875, ((0, 16), (1, 48)), jnp.float32),
        "tile_rows": draw_tile_rows(jax.random.fold_in(arg_keys[6], 71), 0),
        "tile_cols": draw_tile_cols(jax.random.fold_in(arg_keys[6], 71), 0),
    }


def select_rows(indices, length):
    return (indices[..., None] == jnp.arange(length, dtype=jnp.int32)).astype(jnp.float32)


def reference(features, weight, cotangent, tiles, tile_rows, tile_cols):
    highest = lax.Precision.HIGHEST
    block_rows = N_COL * NODE_DEV // BLOCK
    block_cols = N_ROW * NODE_DEV // BLOCK
    grid_view = features.reshape(N_ROW, N_COL, NODE_DEV, FEAT)
    columns = jnp.transpose(grid_view, (1, 0, 2, 3)).reshape(N_COL, block_cols, BLOCK, FEAT)

    def forward_group(inputs):
        group_tiles, group_rows, group_cols = inputs
        col_select = select_rows(group_cols, block_cols)
        row_select = select_rows(group_rows, block_rows)
        blocks = jnp.einsum("csk,ckif->csif", col_select, columns, precision=highest)
        products = jnp.einsum("csij,csjf->csif", group_tiles, blocks, precision=highest)
        summed = jnp.einsum("csb,csif->bif", row_select, products, precision=highest)
        return summed.reshape(N_COL * NODE_DEV, FEAT)

    aggregated = lax.map(forward_group, (tiles, tile_rows, tile_cols)).reshape(NODES, FEAT)
    preact = jnp.dot(aggregated, weight, precision=highest)
    hidden = jnp.tanh(preact)
    delta_pre = cotangent * (1.0 - hidden * hidden)
    grad_weight = jnp.dot(aggregated.T, delta_pre, precision=highest)
    back_rows = jnp.dot(delta_pre, weight.T, precision=highest)
    back_groups = back_rows.reshape(N_ROW, block_rows, BLOCK, FEAT)

    def backward_group(running, inputs):
        group_tiles, group_rows, group_cols, group_back = inputs
        col_select = select_rows(group_cols, block_cols)
        row_select = select_rows(group_rows, block_rows)
        picked = jnp.einsum("csb,bif->csif", row_select, group_back, precision=highest)
        products = jnp.einsum("csji,csjf->csif", group_tiles, picked, precision=highest)
        return running + jnp.einsum("csk,csif->ckif", col_select, products, precision=highest), None

    initial = jnp.zeros((N_COL, block_cols, BLOCK, FEAT), jnp.float32)
    accumulated, unused = lax.scan(backward_group, initial, (tiles, tile_rows, tile_cols, back_groups))
    grad_features = jnp.transpose(accumulated.reshape(N_COL, N_ROW, NODE_DEV, FEAT), (1, 0, 2, 3)).reshape(NODES, FEAT)
    return hidden, grad_features, grad_weight
```

```python
import functools

import jax
import jax.numpy as jnp
from jax import lax
from jax.experimental import pallas as pl
from jax.experimental.pallas import tpu as pltpu
from jax.sharding import PartitionSpec as P

MESH = pl.DeviceIdType.MESH
F32 = jnp.float32
BF16 = jnp.bfloat16
BLK = 128


def split(v):
    high = v.astype(BF16)
    return high, (v - high.astype(F32)).astype(BF16)


def dot3(a, b, dims=((1,), (0,))):
    ah, al = split(a)
    bh, bl = split(b)

    def one(p, q):
        return lax.dot_general(p, q, (dims, ((), ())), preferred_element_type=F32)

    return one(ah, bh) + (one(ah, bl) + one(al, bh))


def layer_kernel(ny, nz, feat, w, cot, tiles, trows, tcols, hid, gfeat, gwo, meta_out, *scratch):
    (halves, xb, sib, meta, prod,
     zs, zr, zqs, zqr, agg, ab, ys, yr, yqs, yqr, fin,
     g0, r1, s1, r2, s2, r3, r4, s4, gout,
     sm, mloc, tq_s, tq_r,
     xq_s, xq_r, xr_s, xr_r, zrs_s, zrs_r, zq_s, zq_r,
     bq_s, bq_r, br_s, br_r, yrs_s, yrs_r, yq_s, yq_r,
     g1_s, g1_r, g2_s, g2_r, g3_s, g3_r, g4_s, g4_r, g5_s, g5_r, g6_s, g6_r) = scratch
    r = lax.axis_index("row")
    c = lax.axis_index("col")
    xh, y = r // ny, r % ny
    z, xl, k = c // 4, (c // 2) % 2, c % 2
    sgn = 1 - 2 * k
    slots = tiles.shape[0]

    def dev(xh_, y_, z_, xl_, k_):
        return (xh_ * ny + y_, z_ * 4 + xl_ * 2 + k_)

    def quad_x(q):
        return dev((xh + q // 2) % 2, y, z, xl, (k + q % 2) % 2)

    def quad_l(q):
        return dev(xh, y, z, (xl + q // 2) % 2, (k + q % 2) % 2)

    def at_y(d):
        return dev(xh, (y + d + ny) % ny, z, xl, k)

    def at_z(d):
        return dev(xh, y, (z + d + nz) % nz, xl, k)

    def remote(src, dst, ss, rs, to):
        return pltpu.make_async_remote_copy(
            src_ref=src, dst_ref=dst, send_sem=ss, recv_sem=rs, device_id=to, device_id_type=MESH)

    peers = [quad_x(1), quad_x(2), quad_x(3), quad_l(2), quad_l(3)]
    peers += [at_y(d) for d in range(1, ny)]
    peers += [at_z(d) for d in range(1, nz)]
    barrier = pltpu.get_barrier_semaphore()
    for to in peers:
        pl.semaphore_signal(barrier, inc=1, device_id=to, device_id_type=MESH)
    pl.semaphore_wait(barrier, len(peers))

    def lane_of(xbit, q):
        return ((xbit + q // 2) % 2) * 2 + (k + q % 2) % 2

    class Gather:
        def __init__(self, buf, src, pos, n, xbit, quad, ring, qs, qr, ss, rs):
            self.__dict__.update(locals())
            self.h = n // 2

        def entry(self, p, q):
            return self.buf.at[((p + 2 * self.n) % self.n) * 4 + lane_of(self.xbit, q)]

        def first(self, q):
            ref = self.entry(self.pos, 0)
            return remote(self.src.at[(k + q % 2) % 2], ref, self.qs.at[q - 1], self.qr.at[q - 1], self.quad(q))

        def first_arrival(self, q):
            ref = self.entry(self.pos, q)
            return remote(ref, ref, self.qs.at[q - 1], self.qr.at[q - 1], self.quad(q))

        def step(self, d, j, q, shift=0):
            way = sgn if d == 0 else -sgn
            ref = self.entry(self.pos - way * (j + shift), q)
            return remote(ref, ref, self.ss.at[d, j, q], self.rs.at[d, j, q], self.ring(way))

        def arrival(self, d, j, q):
            return self.step(d, j, q, 1)

        def start(self):
            for q in (1, 2, 3):
                self.first(q).start()
            idx = self.pos * 4 + lane_of(self.xbit, 0)
            self.buf[pl.ds(idx, 1)] = self.src[pl.ds(k, 1)]
            self.step(0, 0, 0).start()
            self.step(1, 0, 0).start()

        def enter(self):
            for q in (1, 2, 3):
                self.first_arrival(q).wait_recv()
                self.step(0, 0, q).start()
                self.step(1, 0, q).start()

        def forward(self, j):
            for q in range(4):
                for d in (0, 1):
                    self.arrival(d, j - 1, q).wait_recv()
                    if j < self.h - 1 or d == 0:
                        self.step(d, j, q).start()

        def finish(self):
            for q in range(4):
                self.arrival(0, self.h - 1, q).wait_recv()

        def drain(self):
            for q in (1, 2, 3):
                self.first(q).wait_send()

            def both(j, carry):
                for q in range(4):
                    for d in (0, 1):
                        self.step(d, j, q).wait_send()
                return carry

            lax.fori_loop(0, self.h - 1, both, 0)
            for q in range(4):
                self.step(0, self.h - 1, q).wait_send()

    class Scatter:
        def __init__(self, part, first, got, qsend, qgot, pos, n, xbit, quad, ring, ss, rs, qs, qr):
            self.__dict__.update(locals())
            self.h = n // 2

        def own(self, d, j, q):
            ahead = self.h - j if d == 0 else -(self.h - 1 - j)
            p = (self.pos + sgn * ahead + self.n) % self.n
            return self.part(p, lane_of(self.xbit, q))

        def step(self, d, j, q, src):
            way = sgn if d == 0 else -sgn
            return remote(src, self.got.at[d, j, q], self.ss.at[d, j, q], self.rs.at[d, j, q], self.ring(way))

        def arrival(self, d, j, q):
            return self.step(d, j, q, self.got.at[d, j, q])

        def begin(self):
            def lane(q, carry):
                for d in (0, 1):
                    self.first[d, q] = self.own(d, 0, q)
                    self.step(d, 0, q, self.first.at[d, q]).start()
                return carry

            lax.fori_loop(0, 4, lane, 0)

        def pass_on(self, d, j, q):
            value = self.own(d, j, q)
            self.arrival(d, j - 1, q).wait_recv()
            self.got[d, j - 1, q] = self.got[d, j - 1, q] + value
            self.step(d, j, q, self.got.at[d, j - 1, q]).start()

        def run(self):
            self.begin()

            def both(t, carry):
                for d in (0, 1):
                    self.pass_on(d, t // 4 + 1, t % 4)
                return carry

            lax.fori_loop(0, 4 * (self.h - 2), both, 0)

            def last(q, carry):
                self.pass_on(0, self.h - 1, q)
                return carry

            lax.fori_loop(0, 4, last, 0)

        def total(self, q):
            value = self.part(self.pos, lane_of(self.xbit, q))
            self.arrival(1, self.h - 2, q).wait_recv()
            self.arrival(0, self.h - 1, q).wait_recv()
            return value + self.got[0, self.h - 1, q] + self.got[1, self.h - 2, q]

        def handover(self, q, i):
            return remote(self.qsend.at[i], self.qgot.at[i], self.qs.at[i], self.qr.at[i], self.quad(q))

        def finish(self, out):
            for q in (1, 2, 3):
                self.qsend[q - 1] = self.total(q)
                self.handover(q, q - 1).start()
            mine = self.total(0)
            self.handover(2, 1).wait_recv()
            out[pl.ds(k, 1)] = (mine + self.qgot[1])[None]
            self.handover(1, 0).wait_recv()
            self.handover(3, 2).wait_recv()
            out[pl.ds(1 - k, 1)] = (self.qgot[0] + self.qgot[2])[None]

        def drain(self):
            for q in (1, 2, 3):
                self.handover(q, q - 1).wait_send()

            def both(t, carry):
                for d in (0, 1):
                    self.arrival(d, t // 4, t % 4).wait_send()
                return carry

            lax.fori_loop(0, 4 * (self.h - 1), both, 0)
            for q in range(4):
                self.arrival(0, self.h - 1, q).wait_send()

    halves[0] = feat[:, :BLK]
    halves[1] = feat[:, BLK:]
    column = Gather(xb, halves, y, ny, xh, quad_x, at_y, xq_s, xq_r, xr_s, xr_r)
    column.start()
    send_rows = remote(trows, meta_out.at[0], tq_s.at[1], tq_r.at[1], quad_x(1))
    send_cols = remote(tcols, meta_out.at[1], tq_s.at[2], tq_r.at[2], quad_x(1))
    send_rows.start()
    send_cols.start()
    own_rows = pltpu.make_async_copy(trows, sm.at[0], mloc.at[0])
    own_cols = pltpu.make_async_copy(tcols, sm.at[1], mloc.at[1])
    own_rows.start()
    own_cols.start()
    column.enter()
    send_tiles = remote(tiles, sib, tq_s.at[0], tq_r.at[0], quad_x(1))
    send_tiles.start()
    send_rows.wait_recv()
    send_cols.wait_recv()
    own_rows.wait()
    own_cols.wait()
    sib_rows = pltpu.make_async_copy(meta_out.at[0], sm.at[2], mloc.at[2])
    sib_cols = pltpu.make_async_copy(meta_out.at[1], sm.at[3], mloc.at[3])
    sib_rows.start()
    sib_cols.start()
    sib_rows.wait()
    sib_cols.wait()
    for j in range(1, ny // 2):
        column.forward(j)
    send_tiles.wait_recv()
    column.finish()

    tile_of = (tiles, sib)

    def row_at(g, s):
        return sm[2 * g, s]

    def col_at(g, s):
        return sm[2 * g + 1, s]

    def core_of(g):
        return (k + g) % 2

    def products(s, carry):
        for g in (0, 1):
            col = col_at(g, s)
            place = (col % ny) * 4 + (col // ny) * 2 + core_of(g)
            prod[g * slots + s] = dot3(tile_of[g][s], xb[place])
        return carry

    lax.fori_loop(0, slots, products, 0)

    def row_part(p, lane):
        block = p * 4 + lane
        acc = jnp.zeros((BLK, BLK), F32)
        for g in (0, 1):
            for s in range(slots):
                acc = acc + jnp.where(row_at(g, s) == block, 1.0, 0.0) * prod[g * slots + s]
        return acc

    rows = Scatter(row_part, zs, zr, zqs, zqr, z, nz, xl, quad_l, at_z, zrs_s, zrs_r, zq_s, zq_r)
    rows.run()
    rows.finish(agg)

    aggregated = jnp.concatenate([agg[0], agg[1]], axis=1)
    hidden = jnp.tanh(dot3(aggregated, w[...]))
    hid[...] = hidden
    delta = cot[...] * (1.0 - hidden * hidden)
    back = dot3(delta, w[...], ((1,), (1,)))
    column.drain()
    halves[0] = back[:, :BLK]
    halves[1] = back[:, BLK:]
    group = Gather(ab, halves, z, nz, xl, quad_l, at_z, bq_s, bq_r, br_s, br_r)
    group.start()

    g0[...] = dot3(aggregated, delta, ((0,), (0,))).reshape(g0.shape)
    m = lane_of(xl, 0)
    per = g0.shape[0] // ny

    def chunk(p):
        return pl.ds(((p + ny) % ny) * per, per)

    def sum_y(d):
        return remote(g0.at[chunk(y + d)], r1.at[d - 1], g1_s.at[d - 1], g1_r.at[d - 1], at_y(d))

    def sum_quad(q):
        return remote(s1.at[lane_of(xl, q)], r2.at[q - 1], g2_s.at[q - 1], g2_r.at[q - 1], quad_l(q))

    def sum_x():
        return remote(s2, r3, g3_s.at[0], g3_r.at[0], quad_x(2))

    def sum_z(d):
        return remote(s4.at[0], r4.at[z], g4_s.at[d - 1], g4_r.at[d - 1], at_z(d))

    def sum_z_in(d):
        return remote(s4.at[0], r4.at[(z - d + nz) % nz], g4_s.at[d - 1], g4_r.at[d - 1], at_z(d))

    def spread_quad(q, p):
        ref = gout.at[y * per + lane_of(xl, p)]
        return remote(ref, ref, g5_s.at[q - 1], g5_r.at[q - 1], quad_l(q))

    def spread_y(d, back_by):
        ref = gout.at[chunk(y - back_by)]
        return remote(ref, ref, g6_s.at[d - 1], g6_r.at[d - 1], at_y(d))

    for d in range(1, ny):
        sum_y(d).start()
    group.enter()

    group.forward(1)
    acc = g0[chunk(y)]
    for d in range(1, ny):
        sum_y(d).wait_recv()
        acc = acc + r1[d - 1]
    s1[...] = acc
    for q in (1, 2, 3):
        sum_quad(q).start()

    group.forward(2)
    acc = s1[m]
    for q in (1, 2, 3):
        sum_quad(q).wait_recv()
        acc = acc + r2[q - 1]
    s2[...] = acc
    sum_x().start()

    group.forward(3)
    sum_x().wait_recv()
    s4[0] = s2[...] + r3[...]
    for d in range(1, nz):
        sum_z(d).start()
    r4[z] = s4[0]

    group.forward(4)
    for d in range(1, nz):
        sum_z_in(d).wait_recv()
    acc = r4[0]
    for p in range(1, nz):
        acc = acc + r4[p]
    gout[y * per + m] = acc
    for q in (1, 2, 3):
        spread_quad(q, 0).start()

    for j in range(5, nz // 2):
        group.forward(j)
    for q in (1, 2, 3):
        spread_quad(q, q).wait_recv()
    for d in range(1, ny):
        spread_y(d, 0).start()
    group.finish()

    def back_products(s, carry):
        for g in (0, 1):
            row = jnp.maximum(row_at(g, s), 0)
            prod[g * slots + s] = dot3(tile_of[g][s], ab[row], ((0,), (0,)))
        return carry

    lax.fori_loop(0, slots, back_products, 0)

    def col_part(p, lane):
        block = (lane // 2) * ny + p
        acc = jnp.zeros((BLK, BLK), F32)
        g_base = ((lane + k) % 2) * slots
        which = (lane + k) % 2
        for s in range(slots):
            live = (sm[2 * which + 1, s] == block) & (sm[2 * which, s] >= 0)
            acc = acc + jnp.where(live, 1.0, 0.0) * prod[g_base + s]
        return acc

    cols = Scatter(col_part, ys, yr, yqs, yqr, y, ny, xh, quad_x, at_y, yrs_s, yrs_r, yq_s, yq_r)
    cols.run()
    cols.finish(fin)
    gfeat[:, :BLK] = fin[0]
    gfeat[:, BLK:] = fin[1]

    for d in range(1, ny):
        spread_y(d, d).wait_recv()
    gwo[...] = gout[...].reshape(gwo.shape)

    send_tiles.wait_send()
    send_rows.wait_send()
    send_cols.wait_send()
    group.drain()
    rows.drain()
    cols.drain()
    for d in range(1, ny):
        sum_y(d).wait_send()
        spread_y(d, 0).wait_send()
    for q in (1, 2, 3):
        sum_quad(q).wait_send()
        spread_quad(q, 0).wait_send()
    sum_x().wait_send()
    for d in range(1, nz):
        sum_z(d).wait_send()


def on_device(features, weight, cotangent, tiles, tile_rows, tile_cols):
    ny = lax.axis_size("row") // 2
    nz = lax.axis_size("col") // 4
    node_count, width = features.shape
    slots = tiles.shape[2]
    half = (BLK, BLK)
    hy, hz = ny // 2, nz // 2
    lines = width // 8
    per = lines // ny
    dma = pltpu.SemaphoreType.DMA
    vmem = pltpu.VMEM
    scratch = [
        vmem((2,) + half, F32), vmem((ny * 4,) + half, F32), vmem((slots,) + half, F32),
        vmem((8, 128), jnp.int32), vmem((2 * slots,) + half, F32),
        vmem((2, 4) + half, F32), vmem((2, hz, 4) + half, F32), vmem((3,) + half, F32), vmem((3,) + half, F32),
        vmem((2,) + half, F32), vmem((nz * 4,) + half, F32),
        vmem((2, 4) + half, F32), vmem((2, hy, 4) + half, F32), vmem((3,) + half, F32), vmem((3,) + half, F32),
        vmem((2,) + half, F32),
        vmem((lines, 8, width), F32), vmem((ny - 1, per, 8, width), F32), vmem((per, 8, width), F32),
        vmem((3, 8, width), F32), vmem((8, width), F32), vmem((8, width), F32),
        vmem((nz, 8, width), F32), vmem((1, 8, width), F32), vmem((lines, 8, width), F32),
        pltpu.SMEM((4, slots), jnp.int32), dma((4,)), dma((3,)), dma((3,)),
        dma((3,)), dma((3,)), dma((2, hy, 4)), dma((2, hy, 4)),
        dma((2, hz, 4)), dma((2, hz, 4)), dma((3,)), dma((3,)),
        dma((3,)), dma((3,)), dma((2, hz, 4)), dma((2, hz, 4)),
        dma((2, hy, 4)), dma((2, hy, 4)), dma((3,)), dma((3,)),
        dma((ny - 1,)), dma((ny - 1,)), dma((3,)), dma((3,)), dma((1,)), dma((1,)),
        dma((nz - 1,)), dma((nz - 1,)), dma((3,)), dma((3,)), dma((ny - 1,)), dma((ny - 1,)),
    ]
    in_vmem = pl.BlockSpec(memory_space=pltpu.VMEM)
    anywhere = pl.BlockSpec(memory_space=pl.ANY)
    out = pl.pallas_call(
        functools.partial(layer_kernel, ny, nz),
        out_shape=(
            jax.ShapeDtypeStruct((node_count, width), F32),
            jax.ShapeDtypeStruct((node_count, width), F32),
            jax.ShapeDtypeStruct((width, width), F32),
            jax.ShapeDtypeStruct((2, slots), jnp.int32),
        ),
        in_specs=[in_vmem] * 4 + [anywhere] * 2,
        out_specs=(in_vmem, in_vmem, in_vmem, anywhere),
        scratch_shapes=scratch,
        compiler_params=pltpu.CompilerParams(
            collective_id=0, has_side_effects=True, vmem_limit_bytes=40 * 1024 * 1024),
    )(features, weight, cotangent, tiles[0, 0], tile_rows[0, 0], tile_cols[0, 0])
    return out[0], out[1], out[2]


def solution(mesh):
    placed = (
        P(("row", "col"), None),
        P(),
        P(("row", "col"), None),
        P("row", "col", None, None, None),
        P("row", "col", None),
        P("row", "col", None),
    )
    return jax.shard_map(
        on_device,
        mesh=mesh,
        in_specs=placed,
        out_specs=(P(("row", "col"), None), P(("row", "col"), None), P()),
        check_vma=False,
    )
```

```python
import functools

import jax
import jax.numpy as jnp
from jax import lax
from jax.experimental import pallas as pl
from jax.experimental.pallas import tpu as pltpu
from jax.sharding import PartitionSpec as P

MESH = pl.DeviceIdType.MESH
F32 = jnp.float32
BF16 = jnp.bfloat16
BLK = 128
NEAR = 3


def split(v):
    high = v.astype(BF16)
    return high, (v - high.astype(F32)).astype(BF16)


def dot3(a, b, dims=((1,), (0,))):
    ah, al = split(a)
    bh, bl = split(b)

    def one(p, q):
        return lax.dot_general(p, q, (dims, ((), ())), preferred_element_type=F32)

    return one(ah, bh) + (one(ah, bl) + one(al, bh))


def layer_kernel(ny, nz, feat, w_in, cot_in, tiles_in, trows, tcols, hid, gfeat, gwo, meta_out, *scratch):
    (halves, w, cot, tiles, xb, sib, prod,
     zs, zr, zqs, zqr, agg, ab, ys, yr, yqs, yqr, fin,
     g0, r1, s1, r2, s2, r3, r4, s4, gout,
     sm, mloc, tq_s, tq_r, loads,
     xq_s, xq_r, xr_s, xr_r, zrs_s, zrs_r, zq_s, zq_r,
     bq_s, bq_r, br_s, br_r, yrs_s, yrs_r, yq_s, yq_r,
     g1_s, g1_r, g2_s, g2_r, g3_s, g3_r, g4_s, g4_r, g5_s, g5_r, g6_s, g6_r,
     hs, hr, hop_s, hop_r, bx_s, bx_r, pairs) = scratch
    r = lax.axis_index("row")
    c = lax.axis_index("col")
    xh, y = r // ny, r % ny
    z, xl, k = c // 4, (c // 2) % 2, c % 2
    sgn = 1 - 2 * k
    slots = tiles.shape[0]

    def dev(xh_, y_, z_, xl_, k_):
        return (xh_ * ny + y_, z_ * 4 + xl_ * 2 + k_)

    def quad_x(q):
        return dev((xh + q // 2) % 2, y, z, xl, (k + q % 2) % 2)

    def quad_l(q):
        return dev(xh, y, z, (xl + q // 2) % 2, (k + q % 2) % 2)

    def at_y(d):
        return dev(xh, (y + d + ny) % ny, z, xl, k)

    def at_z(d):
        return dev(xh, y, (z + d + nz) % nz, xl, k)

    def remote(src, dst, ss, rs, to):
        return pltpu.make_async_remote_copy(
            src_ref=src, dst_ref=dst, send_sem=ss, recv_sem=rs, device_id=to, device_id_type=MESH)

    peers = [quad_x(1), quad_x(2), quad_x(3), quad_l(2), quad_l(3)]
    peers += [at_y(d) for d in range(1, ny)]
    peers += [at_z(d) for d in range(1, nz)]
    load = [pltpu.make_async_copy(src, dst, loads.at[i]) for i, (src, dst) in enumerate((
        (feat.at[:, pl.ds(0, BLK)], halves.at[0]), (feat.at[:, pl.ds(BLK, BLK)], halves.at[1]),
        (tiles_in, tiles), (w_in, w), (cot_in, cot)))]
    barrier = pltpu.get_barrier_semaphore()
    for to in peers:
        pl.semaphore_signal(barrier, inc=1, device_id=to, device_id_type=MESH)
    for item in load:
        item.start()
    own_rows = pltpu.make_async_copy(trows, sm.at[0], mloc.at[0])
    own_cols = pltpu.make_async_copy(tcols, sm.at[1], mloc.at[1])
    own_rows.start()
    own_cols.start()
    load[0].wait()
    load[1].wait()
    pl.semaphore_wait(barrier, len(peers))

    def lane_of(xbit, q):
        return ((xbit + q // 2) % 2) * 2 + (k + q % 2) % 2

    class Gather:
        def __init__(self, buf, src, pos, n, xbit, quad, ring, qs, qr, ss, rs, near=0, xs=None, xr=None):
            self.__dict__.update(locals())
            self.h = n // 2

        def entry(self, p, q):
            return self.buf.at[((p + 2 * self.n) % self.n) * 4 + lane_of(self.xbit, q)]

        def first(self, q):
            ref = self.entry(self.pos, 0)
            return remote(self.src.at[(k + q % 2) % 2], ref, self.qs.at[q - 1], self.qr.at[q - 1], self.quad(q))

        def first_arrival(self, q):
            ref = self.entry(self.pos, q)
            return remote(ref, ref, self.qs.at[q - 1], self.qr.at[q - 1], self.quad(q))

        def step(self, d, j, q, shift=0):
            way = sgn if d == 0 else -sgn
            ref = self.entry(self.pos - way * (j + shift), q)
            return remote(ref, ref, self.ss.at[d, j, q], self.rs.at[d, j, q], self.ring(way))

        def arrival(self, d, j, q):
            return self.step(d, j, q, 1)

        def relay(self, d, i, q, other=0):
            way = sgn if d == 0 else -sgn
            ref = self.entry(self.pos - way * i, q + other)
            return remote(ref, ref, self.xs.at[d, i - 1, q], self.xr.at[d, i - 1, q], self.quad(2))

        def start(self):
            for q in (1, 3, 2):
                self.first(q).start()
            idx = self.pos * 4 + lane_of(self.xbit, 0)
            self.buf[pl.ds(idx, 1)] = self.src[pl.ds(k, 1)]

        def enter(self, lanes):
            for q in lanes:
                if q:
                    self.first_arrival(q).wait_recv()
                self.step(0, 0, q).start()
                self.step(1, 0, q).start()

        def pass_relays(self, i):
            for q in (0, 1):
                for d in (0, 1):
                    self.relay(d, i, q).start()

        def forward(self, j, lanes):
            for q in lanes:
                for d in (0, 1):
                    if q > 1 and 0 < self.near == j:
                        self.relay(d, j, q - 2, 2).wait_recv()
                    else:
                        self.arrival(d, j - 1, q).wait_recv()
                    if j < self.h - 1 or d == 0:
                        self.step(d, j, q).start()

        def finish(self, lanes):
            for q in lanes:
                self.arrival(0, self.h - 1, q).wait_recv()

        def finish_near(self):
            for q in (2, 3):
                self.first_arrival(q).wait_recv()
                for i in range(1, self.near):
                    for d in (0, 1):
                        self.relay(d, i, q - 2, 2).wait_recv()

        def drain(self):
            for q in (1, 2, 3):
                self.first(q).wait_send()

            def both(j, carry):
                for q in range(4):
                    for d in (0, 1):
                        self.step(d, j, q).wait_send()
                return carry

            def own(j, carry):
                for q in (0, 1):
                    for d in (0, 1):
                        self.step(d, j, q).wait_send()
                        self.relay(d, j + 1, q).wait_send()
                return carry

            if self.near:
                lax.fori_loop(0, self.near, own, 0)
            lax.fori_loop(self.near, self.h - 1, both, 0)
            for q in range(4):
                self.step(0, self.h - 1, q).wait_send()

    class Scatter:
        def __init__(self, part, first, got, qsend, qgot, pos, n, xbit, quad, ring, ss, rs, qs, qr,
                     near=0, xsend=None, xgot=None, xs=None, xr=None):
            self.__dict__.update(locals())
            self.h = n // 2

        def term(self, d, i, q):
            p = (self.pos + (sgn * i if d == 0 else -sgn * i) + self.n) % self.n
            return self.part(p, lane_of(self.xbit, q))

        def step(self, d, j, q, src):
            way = sgn if d == 0 else -sgn
            return remote(src, self.got.at[d, j, q], self.ss.at[d, j, q], self.rs.at[d, j, q], self.ring(way))

        def arrival(self, d, j, q):
            return self.step(d, j, q, self.got.at[d, j, q])

        def hop(self, d, i, q):
            return remote(self.xsend.at[d, i, q], self.xgot.at[d, i, q], self.xs.at[d, i, q],
                          self.xr.at[d, i, q], self.quad(2))

        def lanes(self, body, low, high):
            def lane(q, carry):
                body(q)
                return carry

            lax.fori_loop(low, high, lane, 0)

        def begin(self):
            def body(q):
                for d in (0, 1):
                    self.first[d, q] = self.term(d, self.h - d, q)
                    self.step(d, 0, q, self.first.at[d, q]).start()

            self.lanes(lambda t: body((t + 2) % 4), 0, 4)

        def pass_on(self, d, j, q, hopped=False):
            i = self.h - d - j
            value = self.term(d, i, q)
            if hopped:
                self.hop(d, i, q).wait_recv()
                value = value + self.xgot[d, i, q]
            self.arrival(d, j - 1, q).wait_recv()
            self.got[d, j - 1, q] = self.got[d, j - 1, q] + value
            self.step(d, j, q, self.got.at[d, j - 1, q]).start()

        def hop_alone(self, d, i):
            def body(q):
                self.xsend[d, i, q] = self.term(d, i, q + 2)
                self.hop(d, i, q).start()

            self.lanes(body, 0, 2)

        def hop_sum(self, d):
            i = self.near
            j = self.h - d - i - 1

            def body(q):
                value = self.term(d, i, q + 2)
                self.arrival(d, j, q + 2).wait_recv()
                self.xsend[d, i, q] = self.got[d, j, q + 2] + value
                self.hop(d, i, q).start()

            self.lanes(body, 0, 2)

        def run(self):
            self.begin()

            def both(t, carry):
                for d in (0, 1):
                    self.pass_on(d, t // 4 + 1, (t + 2) % 4)
                return carry

            lax.fori_loop(0, 4 * (self.h - 2), both, 0)
            self.lanes(lambda t: self.pass_on(0, self.h - 1, (t + 2) % 4), 0, 4)

        def run_near(self):
            n, h = self.near, self.h
            self.begin()
            self.hop_alone(0, 0)
            self.hop_alone(1, n - 1)
            for j in range(1, h - 1 - n):
                for low in (2, 0):
                    self.lanes(lambda q: [self.pass_on(d, j, q) for d in (0, 1)], low, low + 2)
            self.hop_alone(0, n - 1)
            j = h - 1 - n
            self.hop_sum(1)
            self.lanes(lambda q: self.pass_on(0, j, q), 2, 4)
            self.lanes(lambda q: self.pass_on(0, j, q), 0, 2)
            self.lanes(lambda q: self.pass_on(1, j, q, True), 0, 2)
            self.hop_sum(0)
            for i in range(n - 2, 0, -1):
                self.hop_alone(1, i)
                self.hop_alone(0, i)
            for j in range(h - n, h - 1):
                self.lanes(lambda q: [self.pass_on(d, j, q, True) for d in (1, 0)], 0, 2)
            self.lanes(lambda q: self.pass_on(0, h - 1, q, True), 0, 2)

        def total(self, q):
            value = self.part(self.pos, lane_of(self.xbit, q))
            if self.near:
                self.hop(0, 0, q).wait_recv()
                value = value + self.xgot[0, 0, q]
            self.arrival(1, self.h - 2, q).wait_recv()
            self.arrival(0, self.h - 1, q).wait_recv()
            return value + self.got[0, self.h - 1, q] + self.got[1, self.h - 2, q]

        def handover(self, q, i):
            return remote(self.qsend.at[i], self.qgot.at[i], self.qs.at[i], self.qr.at[i], self.quad(q))

        def finish(self, out):
            for q in (2, 3, 1):
                self.qsend[q - 1] = self.total(q)
                self.handover(q, q - 1).start()
            mine = self.total(0)
            self.handover(2, 1).wait_recv()
            out[pl.ds(k, 1)] = (mine + self.qgot[1])[None]
            self.handover(1, 0).wait_recv()
            self.handover(3, 2).wait_recv()
            out[pl.ds(1 - k, 1)] = (self.qgot[0] + self.qgot[2])[None]

        def finish_near(self, out):
            self.qsend[0] = self.total(1)
            self.handover(1, 0).start()
            out[pl.ds(k, 1)] = self.total(0)[None]
            self.handover(1, 0).wait_recv()
            out[pl.ds(1 - k, 1)] = self.qgot[pl.ds(0, 1)]

        def drain(self):
            for q in (1, 2, 3) if self.near == 0 else (1,):
                self.handover(q, q - 1).wait_send()
            if self.near:
                for q in (0, 1):
                    self.hop(0, 0, q).wait_send()
                    for d in (0, 1):
                        for i in range(1, self.near + 1):
                            self.hop(d, i, q).wait_send()
            for d in (0, 1):
                for high, low in ((2, 0), (4, 2)):
                    last = self.h - d - (self.near if low else 0)

                    def sent(j, carry):
                        for q in range(low, high):
                            self.arrival(d, j, q).wait_send()
                        return carry

                    lax.fori_loop(0, last, sent, 0)

    def split_tiles(g, src):
        def one(s, carry):
            high, low = split(src[s])
            pairs[g * slots + s] = jnp.concatenate([high, low], axis=1)
            return carry

        lax.fori_loop(0, slots, one, 0)

    def product(pair, block):
        high, low = split(block)
        right = jnp.concatenate([jnp.concatenate([high, high], axis=0),
                                 jnp.concatenate([low, jnp.zeros_like(low)], axis=0)], axis=1)
        both = jnp.dot(pair, right, preferred_element_type=F32)
        return both[:, :BLK] + both[:, BLK:]

    column = Gather(xb, halves, y, ny, xh, quad_x, at_y, xq_s, xq_r, xr_s, xr_r)
    column.start()
    send_rows = remote(trows, meta_out.at[0], tq_s.at[1], tq_r.at[1], quad_x(1))
    send_cols = remote(tcols, meta_out.at[1], tq_s.at[2], tq_r.at[2], quad_x(1))
    send_rows.start()
    send_cols.start()
    send_tiles = remote(tiles_in, sib, tq_s.at[0], tq_r.at[0], quad_x(1))
    column.enter((0, 1))
    send_tiles.start()
    send_rows.wait_recv()
    send_cols.wait_recv()
    own_rows.wait()
    own_cols.wait()
    sib_rows = pltpu.make_async_copy(meta_out.at[0], sm.at[2], mloc.at[2])
    sib_cols = pltpu.make_async_copy(meta_out.at[1], sm.at[3], mloc.at[3])
    sib_rows.start()
    sib_cols.start()
    sib_rows.wait()
    sib_cols.wait()
    column.forward(1, (0, 1))
    column.enter((2, 3))
    load[2].wait()
    split_tiles(0, tiles)
    for j in range(2, ny // 2):
        column.forward(j, (0, 1))
        column.forward(j - 1, (2, 3))
    send_tiles.wait_recv()
    split_tiles(1, sib)
    column.finish((0, 1))
    column.forward(ny // 2 - 1, (2, 3))
    column.finish((2, 3))

    def row_at(g, s):
        return sm[2 * g, s]

    def col_at(g, s):
        return sm[2 * g + 1, s]

    def core_of(g):
        return (k + g) % 2

    def products(s, carry):
        for g in (0, 1):
            col = col_at(g, s)
            place = (col % ny) * 4 + (col // ny) * 2 + core_of(g)
            prod[g * slots + s] = product(pairs[g * slots + s], xb[place])
        return carry

    lax.fori_loop(0, slots, products, 0)

    def row_part(p, lane):
        block = p * 4 + lane
        acc = jnp.zeros((BLK, BLK), F32)
        for g in (0, 1):
            for s in range(slots):
                acc = acc + jnp.where(row_at(g, s) == block, 1.0, 0.0) * prod[g * slots + s]
        return acc

    rows = Scatter(row_part, zs, zr, zqs, zqr, z, nz, xl, quad_l, at_z, zrs_s, zrs_r, zq_s, zq_r,
                   NEAR, hs, hr, hop_s, hop_r)
    rows.run_near()
    rows.finish_near(agg)

    load[3].wait()
    load[4].wait()
    aggregated = jnp.concatenate([agg[0], agg[1]], axis=1)
    hidden = jnp.tanh(dot3(aggregated, w[...]))
    hid[...] = hidden
    delta = cot[...] * (1.0 - hidden * hidden)
    back = dot3(delta, w[...], ((1,), (1,)))
    column.drain()
    halves[0] = back[:, :BLK]
    halves[1] = back[:, BLK:]
    group = Gather(ab, halves, z, nz, xl, quad_l, at_z, bq_s, bq_r, br_s, br_r, NEAR, bx_s, bx_r)
    group.start()

    def turn_tiles(g, src):
        def one(s, carry):
            high, low = split(src[s].T)
            pairs[g * slots + s] = jnp.concatenate([high, low], axis=1)
            return carry

        lax.fori_loop(0, slots, one, 0)

    g0[...] = dot3(aggregated, delta, ((0,), (0,))).reshape(g0.shape)
    m = lane_of(xl, 0)
    per = g0.shape[0] // ny

    def chunk(p):
        return pl.ds(((p + ny) % ny) * per, per)

    def sum_y(d):
        return remote(g0.at[chunk(y + d)], r1.at[d - 1], g1_s.at[d - 1], g1_r.at[d - 1], at_y(d))

    def sum_quad(q):
        return remote(s1.at[lane_of(xl, q)], r2.at[q - 1], g2_s.at[q - 1], g2_r.at[q - 1], quad_l(q))

    def sum_x():
        return remote(s2, r3, g3_s.at[0], g3_r.at[0], quad_x(2))

    def sum_z(d):
        return remote(s4.at[0], r4.at[z], g4_s.at[d - 1], g4_r.at[d - 1], at_z(d))

    def sum_z_in(d):
        return remote(s4.at[0], r4.at[(z - d + nz) % nz], g4_s.at[d - 1], g4_r.at[d - 1], at_z(d))

    def spread_quad(q, p):
        ref = gout.at[y * per + lane_of(xl, p)]
        return remote(ref, ref, g5_s.at[q - 1], g5_r.at[q - 1], quad_l(q))

    def spread_y(d, back_by):
        ref = gout.at[chunk(y - back_by)]
        return remote(ref, ref, g6_s.at[d - 1], g6_r.at[d - 1], at_y(d))

    for d in range(1, ny):
        sum_y(d).start()
    group.enter((0, 1))

    group.forward(1, (0, 1))
    group.pass_relays(1)
    turn_tiles(0, tiles)
    acc = g0[chunk(y)]
    for d in range(1, ny):
        sum_y(d).wait_recv()
        acc = acc + r1[d - 1]
    s1[...] = acc
    for q in (1, 2, 3):
        sum_quad(q).start()

    group.forward(2, (0, 1))
    turn_tiles(1, sib)
    acc = s1[m]
    for q in (1, 2, 3):
        sum_quad(q).wait_recv()
        acc = acc + r2[q - 1]
    s2[...] = acc
    sum_x().start()

    group.forward(3, (0, 1))
    group.pass_relays(3)
    group.pass_relays(2)
    sum_x().wait_recv()
    s4[0] = s2[...] + r3[...]
    for d in range(1, nz):
        sum_z(d).start()
    r4[z] = s4[0]

    group.forward(4, (0, 1))
    group.forward(3, (2, 3))
    for d in range(1, nz):
        sum_z_in(d).wait_recv()
    acc = r4[0]
    for p in range(1, nz):
        acc = acc + r4[p]
    gout[y * per + m] = acc
    for q in (1, 2, 3):
        spread_quad(q, 0).start()

    group.forward(5, (0, 1))
    group.forward(4, (2, 3))
    for q in (1, 2, 3):
        spread_quad(q, q).wait_recv()
    for d in range(1, ny):
        spread_y(d, 0).start()
    group.finish((0, 1))
    group.forward(5, (2, 3))
    group.finish((2, 3))
    group.finish_near()

    def back_products(s, carry):
        for g in (0, 1):
            row = jnp.maximum(row_at(g, s), 0)
            prod[g * slots + s] = product(pairs[g * slots + s], ab[row])
        return carry

    lax.fori_loop(0, slots, back_products, 0)

    def col_part(p, lane):
        block = (lane // 2) * ny + p
        acc = jnp.zeros((BLK, BLK), F32)
        g_base = ((lane + k) % 2) * slots
        which = (lane + k) % 2
        for s in range(slots):
            live = (sm[2 * which + 1, s] == block) & (sm[2 * which, s] >= 0)
            acc = acc + jnp.where(live, 1.0, 0.0) * prod[g_base + s]
        return acc

    cols = Scatter(col_part, ys, yr, yqs, yqr, y, ny, xh, quad_x, at_y, yrs_s, yrs_r, yq_s, yq_r)
    cols.run()
    cols.finish(fin)
    gfeat[:, :BLK] = fin[0]
    gfeat[:, BLK:] = fin[1]

    for d in range(1, ny):
        spread_y(d, d).wait_recv()
    gwo[...] = gout[...].reshape(gwo.shape)

    send_tiles.wait_send()
    send_rows.wait_send()
    send_cols.wait_send()
    group.drain()
    rows.drain()
    cols.drain()
    for d in range(1, ny):
        sum_y(d).wait_send()
        spread_y(d, 0).wait_send()
    for q in (1, 2, 3):
        sum_quad(q).wait_send()
        spread_quad(q, 0).wait_send()
    sum_x().wait_send()
    for d in range(1, nz):
        sum_z(d).wait_send()


def on_device(features, weight, cotangent, tiles, tile_rows, tile_cols):
    ny = lax.axis_size("row") // 2
    nz = lax.axis_size("col") // 4
    node_count, width = features.shape
    slots = tiles.shape[2]
    half = (BLK, BLK)
    hy, hz = ny // 2, nz // 2
    lines = width // 8
    per = lines // ny
    dma = pltpu.SemaphoreType.DMA
    vmem = pltpu.VMEM
    scratch = [
        vmem((2,) + half, F32), vmem((width, width), F32), vmem((node_count, width), F32),
        vmem((slots,) + half, F32), vmem((ny * 4,) + half, F32), vmem((slots,) + half, F32),
        vmem((2 * slots,) + half, F32),
        vmem((2, 4) + half, F32), vmem((2, hz, 4) + half, F32), vmem((3,) + half, F32), vmem((3,) + half, F32),
        vmem((2,) + half, F32), vmem((nz * 4,) + half, F32),
        vmem((2, 4) + half, F32), vmem((2, hy, 4) + half, F32), vmem((3,) + half, F32), vmem((3,) + half, F32),
        vmem((2,) + half, F32),
        vmem((lines, 8, width), F32), vmem((ny - 1, per, 8, width), F32), vmem((per, 8, width), F32),
        vmem((3, 8, width), F32), vmem((8, width), F32), vmem((8, width), F32),
        vmem((nz, 8, width), F32), vmem((1, 8, width), F32), vmem((lines, 8, width), F32),
        pltpu.SMEM((4, slots), jnp.int32), dma((4,)), dma((3,)), dma((3,)),
        dma((5,)),
        dma((3,)), dma((3,)), dma((2, hy, 4)), dma((2, hy, 4)),
        dma((2, hz, 4)), dma((2, hz, 4)), dma((3,)), dma((3,)),
        dma((3,)), dma((3,)), dma((2, hz, 4)), dma((2, hz, 4)),
        dma((2, hy, 4)), dma((2, hy, 4)), dma((3,)), dma((3,)),
        dma((ny - 1,)), dma((ny - 1,)), dma((3,)), dma((3,)), dma((1,)), dma((1,)),
        dma((nz - 1,)), dma((nz - 1,)), dma((3,)), dma((3,)), dma((ny - 1,)), dma((ny - 1,)),
        vmem((2, NEAR + 1, 2) + half, F32), vmem((2, NEAR + 1, 2) + half, F32),
        dma((2, NEAR + 1, 2)), dma((2, NEAR + 1, 2)), dma((2, NEAR, 2)), dma((2, NEAR, 2)),
        vmem((2 * slots, BLK, 2 * BLK), BF16),
    ]
    in_vmem = pl.BlockSpec(memory_space=pltpu.VMEM)
    in_hbm = pl.BlockSpec(memory_space=pltpu.HBM)
    out = pl.pallas_call(
        functools.partial(layer_kernel, ny, nz),
        out_shape=(
            jax.ShapeDtypeStruct((node_count, width), F32),
            jax.ShapeDtypeStruct((node_count, width), F32),
            jax.ShapeDtypeStruct((width, width), F32),
            jax.ShapeDtypeStruct((2, slots), jnp.int32),
        ),
        in_specs=[in_hbm] * 6,
        out_specs=(in_vmem, in_vmem, in_vmem, in_hbm),
        scratch_shapes=scratch,
        compiler_params=pltpu.CompilerParams(
            collective_id=0, has_side_effects=True, vmem_limit_bytes=62 * 1024 * 1024),
    )(features, weight, cotangent, tiles[0, 0], tile_rows[0, 0], tile_cols[0, 0])
    return out[0], out[1], out[2]


def solution(mesh):
    placed = (
        P(("row", "col"), None),
        P(),
        P(("row", "col"), None),
        P("row", "col", None, None, None),
        P("row", "col", None),
        P("row", "col", None),
    )
    return jax.shard_map(
        on_device,
        mesh=mesh,
        in_specs=placed,
        out_specs=(P(("row", "col"), None), P(("row", "col"), None), P()),
        check_vma=False,
    )
```
